32 devices in a mesh: dp: 8 (over y, x, core), slab: 4 (over z).
Axes of the slice: x: 2, y: 2, z: 4, core: 2. Of those that a mesh axis runs over, the one named last changes fastest.
Arguments:
- features: bfloat16 [8, 8, 16, 16, 256], P('dp', 'slab'), may hold values from -6 to 6
- kernel: bfloat16 [27, 256, 256], replicated, may hold values from -6 to 6
- head_proj: bfloat16 [256, 2], replicated, may hold values from -0.375 to 0.375
- material_ids: int32 [8, 8, 16, 16], P('dp', 'slab'), may hold values from 0 to 3
- port_ids: int32 [8, 8, 16, 16], P('dp', 'slab'), may hold values from 0 to 2
- permittivity: float32 [2, 4], replicated, may hold values from 0.2 to 12
- port_source: float32 [2, 2], replicated, may hold values from -4 to 4
- master: float32 [1769472], P(('dp', 'slab')), may hold values from -0.6 to 0.6
- moment: float32 [1769472], P(('dp', 'slab')), may hold values from -0.06 to 0.06
- second: float32 [1769472], P(('dp', 'slab')), may hold values from 1e-05 to 0.001
Outputs:
- new_master: float32 [1769472], P(('dp', 'slab'))
- new_moment: float32 [1769472], P(('dp', 'slab'))
- new_second: float32 [1769472], P(('dp', 'slab'))
- new_kernel: bfloat16 [27, 256, 256], replicated
The draws below stay inside these ranges and needn't reach their ends.
All inputs are finite; a program needn't handle non-finite values.
Results may differ from the reference program's by a relative error of at most 0.0034.
Values may be sent and summed in bfloat16 or wider, within the bound.
A program may use at most 64 MiB of HBM per device.

```python
import math
import jax
import jax.numpy as jnp
from jax import lax

C = 256
TAPS = 27
MATS = 4
PORTS = 2
GRID_H = 16
GRID_W = 16
CROPS = 8
NZ = 8
CELLS = 16384
PARAMS = 1769472


def place_ends(values, stream_key, smallest, largest):
    longest = values.shape.index(max(values.shape))
    spots = []
    for shift in (0, 1):
        where = [jax.random.randint(jax.random.fold_in(stream_key, axis), (), 0, length) for axis, length in enumerate(values.shape)]
        where[longest] = (where[longest] + shift) % values.shape[longest]
        spots.append(tuple(where))
    return values.at[spots[0]].set(smallest).at[spots[1]].set(largest)


def spiked(result, key, source, target, shards_of, factor):
    def block_of(axis_at):
        return (jnp.arange(result.shape[axis_at]) // (result.shape[axis_at] // shards_of)).reshape((-1,) + (1,) * (result.ndim - 1 - axis_at))

    first = jax.random.permutation(key, shards_of)[block_of(target)]
    second = (block_of(target) + shards_of // 2) % shards_of
    return jnp.where((block_of(source) == first) | (block_of(source) == second), factor * result, result)


def steps_of(rng, dims, shards, smallest, high):
    def one(position, blocks):
        draws = jax.random.uniform(jax.random.fold_in(jax.random.fold_in(rng, 6), position), (blocks,), jnp.float32, smallest / len(shards), high / len(shards))
        return jnp.repeat(jnp.exp(draws), dims[position] // blocks).reshape((-1,) + (1,) * (len(dims) - position - 1))

    level = one(*shards[0])
    for cut in shards[1:]:
        level = level * one(*cut)
    return level


def gaussian(stream_key, shape, width, bound, split=(), held_as=jnp.bfloat16):
    array = jax.random.normal(stream_key, shape, jnp.float32) * width
    if len(split) > 0:
        array = steps_of(stream_key, shape, split, -0.22, 0.18) * array
    return jnp.clip(array, min=-bound, max=bound).astype(held_as)


def gaussian_with(rng, shape, spread, reach, split, heavy, held_as=jnp.bfloat16):
    drawn = spread * jax.random.normal(rng, shape, jnp.float32)
    if split:
        drawn = drawn * steps_of(rng, shape, split, -0.22, 0.18)
    return jnp.clip(spiked(drawn, jax.random.fold_in(rng, 3), *heavy), -reach, reach).astype(held_as)


def setup_inputs(seed: int = 0) -> dict:
    key_of = jax.random.split(jax.random.key(seed), 11)
    features = gaussian_with(key_of[0], (CROPS, NZ, GRID_H, GRID_W, C), 1.0, 6.0, ((0, 8), (1, 4)), (0, 4, 8, 2.0))
    kernel = gaussian(key_of[1], (TAPS, C, C), 1.0, 6.0)
    head_proj = gaussian(key_of[2], (C, 2), C ** -0.5, 0.375)
    material_ids = place_ends(jax.random.randint(key_of[3], (CROPS, NZ, GRID_H, GRID_W), 0, MATS), jax.random.fold_in(key_of[3], 1), 0, MATS - 1).astype(jnp.int32)
    port_ids = place_ends(jax.random.randint(key_of[4], (CROPS, NZ, GRID_H, GRID_W), 0, PORTS + 1), jax.random.fold_in(key_of[4], 1), 0, PORTS).astype(jnp.int32)
    permittivity = jnp.clip(jnp.exp(jax.random.uniform(key_of[5], (2, MATS), jnp.float32, math.log(0.2), math.log(12.0))), 0.2, 12.0)
    port_source = gaussian(key_of[6], (2, PORTS), 1.0, 4.0, (), jnp.float32)
    master = gaussian(key_of[7], (PARAMS,), 0.1, 0.6, ((0, 32),), jnp.float32)
    moment = gaussian(key_of[8], (PARAMS,), 0.01, 0.06, ((0, 32),), jnp.float32)
    second = jnp.clip(jnp.exp(math.log(0.001) - 4.6051703 * jax.random.uniform(key_of[9], (PARAMS,), jnp.float32) ** steps_of(key_of[9], (PARAMS,), ((0, 32),), -0.2, 0.2)), 9.999999747378752e-06, 0.001)
    return {"features": features, "kernel": kernel, "head_proj": head_proj, "material_ids": material_ids, "port_ids": port_ids, "permittivity": permittivity, "port_source": port_source, "master": master, "moment": moment, "second": second}


wave_sq = 0.3
beta_one = 0.9
beta_two = 0.99
learn_rate = 0.01
adam_eps = 1e-08

def laplace(extended):
    padded = jnp.pad(extended, ((0, 0), (1, 1), (1, 1), (0, 0)))
    centre = padded[1:-1, 1:-1, 1:-1]
    near = padded[2:, 1:-1, 1:-1] + padded[:-2, 1:-1, 1:-1]
    near = near + padded[1:-1, 2:, 1:-1] + padded[1:-1, :-2, 1:-1]
    near = near + padded[1:-1, 1:-1, 2:] + padded[1:-1, 1:-1, :-2]
    return near - 6.0 * centre

def lookup(codes, table, offset):
    count = table.shape[1]
    values = jnp.arange(count, dtype=jnp.int32) + offset
    hits = codes[..., None] == values
    real_part = lax.optimization_barrier(jnp.sum(jnp.where(hits, table[0], 0.0), axis=-1))
    imag_part = lax.optimization_barrier(jnp.sum(jnp.where(hits, table[1], 0.0), axis=-1))
    return (real_part, imag_part)

def crop_grad(feats, kernel, head_proj, mats, ports, permittivity, port_source):
    slab_depth, grid_rows, grid_cols, channels = feats.shape
    cell_count = slab_depth * grid_rows * grid_cols
    weight_scale = 1.0 / jnp.sqrt(jnp.float32(TAPS * channels))
    padded = jnp.pad(feats, ((1, 1), (1, 1), (1, 1), (0, 0)))
    pieces = []
    summed = jnp.zeros((cell_count, channels), jnp.float32)
    for tap_index in range(27):
        shift_z, shift_y, shift_x = (tap_index // 9, tap_index // 3 % 3, tap_index % 3)
        partial_rows = padded[shift_z:shift_z + slab_depth, shift_y:shift_y + grid_rows, shift_x:shift_x + grid_cols].reshape(cell_count, channels)
        pieces.append(partial_rows)
        summed = summed + jnp.dot(partial_rows, kernel[tap_index], preferred_element_type=jnp.float32)
    preact = summed * weight_scale
    hidden = jax.nn.silu(preact).astype(jnp.bfloat16)
    field_vals = jnp.dot(hidden, head_proj, preferred_element_type=jnp.float32).reshape(slab_depth, grid_rows, grid_cols, 2)
    eps_re, eps_im = lookup(mats, permittivity, 0)
    src_re, src_im = lookup(ports, port_source, 1)
    field_ext = jnp.pad(field_vals, ((1, 1), (0, 0), (0, 0), (0, 0)))
    lap_field = laplace(field_ext)
    field_re, field_im = (field_vals[..., 0], field_vals[..., 1])
    res_re = lap_field[..., 0] + wave_sq * (eps_re * field_re - eps_im * field_im) - src_re
    res_im = lap_field[..., 1] + wave_sq * (eps_re * field_im + eps_im * field_re) - src_im
    norm_scale = 2.0 / jnp.sqrt(jnp.float32(CELLS))
    adj = jnp.stack([res_re * norm_scale, res_im * norm_scale], axis=-1)
    adj_ext = jnp.pad(adj, ((1, 1), (0, 0), (0, 0), (0, 0)))
    lap_adj = laplace(adj_ext)
    grad_re = lap_adj[..., 0] + wave_sq * (eps_re * adj[..., 0] + eps_im * adj[..., 1])
    grad_im = lap_adj[..., 1] + wave_sq * (eps_re * adj[..., 1] - eps_im * adj[..., 0])
    grad_field = jnp.stack([grad_re, grad_im], axis=-1).reshape(cell_count, 2)
    d_hidden = jnp.dot(grad_field, head_proj.astype(jnp.float32).T, precision=lax.Precision.HIGHEST)
    sigma = jax.nn.sigmoid(preact)
    d_pre = (d_hidden * sigma * (1.0 + preact * (1.0 - sigma))).astype(jnp.bfloat16)
    grads = []
    for tap_index in range(27):
        grads.append(lax.dot_general(pieces[tap_index], d_pre, (((0,), (0,)), ((), ())), preferred_element_type=jnp.float32))
    return jnp.stack(grads, axis=0) * weight_scale

def reference(features, kernel, head_proj, material_ids, port_ids, permittivity, port_source, master, moment, second):

    def step(carry, items):
        feats, mats, ports = items
        return (carry + crop_grad(feats, kernel, head_proj, mats, ports, permittivity, port_source), None)
    start = jnp.zeros(kernel.shape, jnp.float32)
    total, _ = lax.scan(step, start, (features, material_ids, port_ids))
    grad = total.reshape(-1)
    new_moment = beta_one * moment + (1.0 - beta_one) * grad
    new_second = beta_two * second + (1.0 - beta_two) * grad * grad
    new_master = master - learn_rate * new_moment / (jnp.sqrt(new_second) + adam_eps)
    new_kernel = new_master.astype(jnp.bfloat16).reshape(kernel.shape)
    return (new_master, new_moment, new_second, new_kernel)
```

```python
import functools

import jax
import jax.numpy as jnp
import numpy as np
from jax import lax
from jax.experimental import pallas as pl
from jax.experimental.pallas import tpu as pltpu
from jax.sharding import PartitionSpec as P

wave_sq = 0.3
beta_one = 0.9
beta_two = 0.99
learn_rate = 0.01
adam_eps = 1e-08


def padded_2(block, sides, width):
    for axis, dim in sides:
        count = lax.axis_size(axis)
        forward = [(i, i + 1) for i in range(count - 1)]
        backward = [(target, source) for source, target in forward]
        low = lax.ppermute(
            lax.slice_in_dim(block, block.shape[dim] - width, None, axis=dim), axis, forward
        )
        high = lax.ppermute(lax.slice_in_dim(block, 0, width, axis=dim), axis, backward)
        block = jnp.concatenate([low, block, high], axis=dim)
    return block


def laplace(extended):
    padded = jnp.pad(extended, ((0, 0), (1, 1), (1, 1), (0, 0)))
    centre = padded[1:-1, 1:-1, 1:-1]
    near = padded[2:, 1:-1, 1:-1] + padded[:-2, 1:-1, 1:-1]
    near = near + padded[1:-1, 2:, 1:-1] + padded[1:-1, :-2, 1:-1]
    near = near + padded[1:-1, 1:-1, 2:] + padded[1:-1, 1:-1, :-2]
    return near - 6.0 * centre


def lookup(codes, table, offset):
    count = table.shape[1]
    values = jnp.arange(count, dtype=jnp.int32) + offset
    hits = codes[..., None] == values
    real_part = jnp.sum(jnp.where(hits, table[0], 0.0), axis=-1)
    imag_part = jnp.sum(jnp.where(hits, table[1], 0.0), axis=-1)
    return (real_part, imag_part)


def widen(block, rows):
    extra = rows - block.shape[0]
    if extra:
        block = jnp.concatenate([block, jnp.zeros((extra, block.shape[1]), block.dtype)], axis=0)
    return block.astype(jnp.bfloat16)


def share_kernel(
    scale,
    grad,
    master,
    moment,
    second,
    new_master,
    new_moment,
    new_second,
    full,
    pair_in,
    group_out,
    group_in,
    line_out,
    line_in,
    narrow,
    pair_send,
    pair_recv,
    group_send,
    group_recv,
    line_send,
    line_recv,
    line_back_send,
    line_back_recv,
    group_back_send,
    group_back_recv,
    pair_back_send,
    pair_back_recv,
):
    groups, _, line, rows, width = grad.shape
    padded = full.shape[3]
    dp = lax.axis_index("dp")
    here = lax.axis_index("slab")
    mine = dp // 2
    core = dp % 2
    sibling = (mine * 2 + 1 - core, here)

    def group_at(step):
        return (mine + step + groups) % groups

    def slab_at(step):
        return (here + step + line) % line

    def group_device(step):
        return (group_at(step) * 2 + core, here)

    def line_device(step):
        return (dp, slab_at(step))

    def remote(source, target, send, recv, device):
        return pltpu.make_async_remote_copy(
            src_ref=source,
            dst_ref=target,
            send_sem=send,
            recv_sem=recv,
            device_id=device,
            device_id_type=pl.DeviceIdType.MESH,
        )

    def pair_copy(k):
        return remote(
            grad.at[group_at(k), 1 - core], pair_in.at[k], pair_send.at[k], pair_recv.at[k], sibling
        )

    def group_copy(k, j):
        return remote(
            group_out.at[k - 1, j],
            group_in.at[k - 1, j],
            group_send.at[k - 1, j],
            group_recv.at[k - 1, j],
            group_device(k),
        )

    def line_copy(j):
        return remote(
            line_out.at[j - 1], line_in.at[j - 1], line_send.at[j - 1], line_recv.at[j - 1], line_device(j)
        )

    def line_back(j):
        spot = full.at[mine, core, here]
        return remote(spot, spot, line_back_send.at[j - 1], line_back_recv.at[j - 1], line_device(j))

    def group_back(k, j):
        spot = full.at[mine, core, slab_at(-j)]
        return remote(
            spot, spot, group_back_send.at[k - 1, j], group_back_recv.at[k - 1, j], group_device(k)
        )

    def pair_back(k, j):
        spot = full.at[group_at(-k), core, slab_at(-j)]
        return remote(spot, spot, pair_back_send.at[k, j], pair_back_recv.at[k, j], sibling)

    others = [sibling]
    others += [group_device(k) for k in range(1, groups)]
    others += [line_device(j) for j in range(1, line)]
    barrier = pltpu.get_barrier_semaphore()
    for device in others:
        pl.semaphore_signal(barrier, inc=1, device_id=device, device_id_type=pl.DeviceIdType.MESH)
    pl.semaphore_wait(barrier, len(others))

    group_order = list(range(1, groups)) + [0]
    line_order = list(range(1, line)) + [0]
    for k in group_order:
        pair_copy(k).start()
    for k in group_order[:-1]:
        pair_copy(k).wait_recv()
        for j in line_order:
            slab = slab_at(j)
            group_out[k - 1, j] = widen(grad[group_at(k), core, slab] + pair_in[k, slab], padded)
            group_copy(k, j).start()
    pair_copy(0).wait_recv()
    total = None
    for j in line_order:
        slab = slab_at(j)
        total = grad[mine, core, slab] + pair_in[0, slab]
        for k in range(1, groups):
            group_copy(k, j).wait_recv()
            total = total + group_in[k - 1, j].astype(jnp.float32)[:rows]
        if j:
            line_out[j - 1] = widen(total, padded)
            line_copy(j).start()
    for j in range(1, line):
        line_copy(j).wait_recv()
        total = total + line_in[j - 1].astype(jnp.float32)[:rows]

    total = total * scale
    parts = width // 128
    for part in range(parts):
        narrow[pl.ds(part, rows, stride=parts), :] = total[:, part * 128 : part * 128 + 128]
    share = narrow[...]
    stepped = beta_one * moment[...] + (1.0 - beta_one) * share
    squared = beta_two * second[...] + (1.0 - beta_two) * share * share
    updated = master[...] - learn_rate * stepped / (jnp.sqrt(squared) + adam_eps)
    new_moment[...] = stepped
    new_second[...] = squared
    new_master[...] = updated
    narrow[...] = updated
    block = jnp.concatenate(
        [narrow[pl.ds(part, rows, stride=parts), :] for part in range(parts)], axis=1
    )
    full[mine, core, here] = widen(block, padded)

    for j in range(1, line):
        line_back(j).start()
    for k in range(1, groups):
        group_back(k, 0).start()
    pair_back(0, 0).start()
    for j in range(1, line):
        line_back(j).wait_recv()
        for k in range(1, groups):
            group_back(k, j).start()
        pair_back(0, j).start()
    for j in range(line):
        for k in range(1, groups):
            group_back(k, j).wait_recv()
            pair_back(k, j).start()
    for j in range(line):
        for k in range(groups):
            pair_back(k, j).wait_recv()
    for k in range(groups):
        pair_copy(k).wait_send()
        for j in range(line):
            pair_back(k, j).wait_send()
            if k:
                group_copy(k, j).wait_send()
                group_back(k, j).wait_send()
    for j in range(1, line):
        line_copy(j).wait_send()
        line_back(j).wait_send()


def share_and_step(grad, master, moment, second, scale):
    rows_all, width = grad.shape
    groups = lax.axis_size("dp") // 2
    line = lax.axis_size("slab")
    rows = rows_all // (groups * 2 * line)
    padded = -(-rows // 16) * 16
    flat = (master.size // 128, 128)
    vmem = pl.BlockSpec(memory_space=pltpu.VMEM)
    dma = pltpu.SemaphoreType.DMA
    state = jax.ShapeDtypeStruct(flat, jnp.float32)
    out = pl.pallas_call(
        functools.partial(share_kernel, scale),
        out_shape=[
            state,
            state,
            state,
            jax.ShapeDtypeStruct((groups, 2, line, padded, width), jnp.bfloat16),
        ],
        in_specs=[vmem] * 4,
        out_specs=[vmem] * 4,
        scratch_shapes=[
            pltpu.VMEM((groups, line, rows, width), jnp.float32),
            pltpu.VMEM((groups - 1, line, padded, width), jnp.bfloat16),
            pltpu.VMEM((groups - 1, line, padded, width), jnp.bfloat16),
            pltpu.VMEM((line - 1, padded, width), jnp.bfloat16),
            pltpu.VMEM((line - 1, padded, width), jnp.bfloat16),
            pltpu.VMEM(flat, jnp.float32),
            dma((groups,)),
            dma((groups,)),
            dma((groups - 1, line)),
            dma((groups - 1, line)),
            dma((line - 1,)),
            dma((line - 1,)),
            dma((line - 1,)),
            dma((line - 1,)),
            dma((groups - 1, line)),
            dma((groups - 1, line)),
            dma((groups, line)),
            dma((groups, line)),
        ],
        compiler_params=pltpu.CompilerParams(
            collective_id=0, has_side_effects=True, vmem_limit_bytes=48 * 1024 * 1024
        ),
    )(
        grad.reshape(groups, 2, line, rows, width),
        master.reshape(flat),
        moment.reshape(flat),
        second.reshape(flat),
    )
    full = out[3][:, :, :, :rows].reshape(rows_all, width)
    return [part.reshape(-1) for part in out[:3]] + [full]


def body(
    features,
    kernel,
    head_proj,
    material_ids,
    port_ids,
    permittivity,
    port_source,
    master,
    moment,
    second,
):
    feats = features[0]
    slab_depth, grid_rows, grid_cols, channels = feats.shape
    cell_count = slab_depth * grid_rows * grid_cols
    all_cells = cell_count * lax.axis_size("dp") * lax.axis_size("slab")
    weight_scale = 1.0 / jnp.sqrt(jnp.float32(27 * channels))
    with_rim = padded_2(features, (("slab", 1),), 1)[0]
    padded = jnp.pad(with_rim, ((0, 0), (1, 1), (1, 1), (0, 0)))
    pieces = []
    summed = jnp.zeros((cell_count, channels), jnp.float32)
    for tap_index in range(27):
        shift_z, shift_y, shift_x = (tap_index // 9, tap_index // 3 % 3, tap_index % 3)
        partial_rows = padded[
            shift_z : shift_z + slab_depth,
            shift_y : shift_y + grid_rows,
            shift_x : shift_x + grid_cols,
        ].reshape(cell_count, channels)
        pieces.append(partial_rows)
        summed = summed + jnp.dot(
            partial_rows, kernel[tap_index], preferred_element_type=jnp.float32
        )
    preact = summed * weight_scale
    hidden = jax.nn.silu(preact).astype(jnp.bfloat16)
    field_vals = jnp.dot(hidden, head_proj, preferred_element_type=jnp.float32).reshape(
        slab_depth, grid_rows, grid_cols, 2
    )
    eps_re, eps_im = lookup(material_ids[0], permittivity, 0)
    src_re, src_im = lookup(port_ids[0], port_source, 1)
    field_ext = padded_2(field_vals, (("slab", 0),), 1)
    lap_field = laplace(field_ext)
    field_re, field_im = (field_vals[..., 0], field_vals[..., 1])
    res_re = lap_field[..., 0] + wave_sq * (eps_re * field_re - eps_im * field_im) - src_re
    res_im = lap_field[..., 1] + wave_sq * (eps_re * field_im + eps_im * field_re) - src_im
    norm_scale = 2.0 / jnp.sqrt(jnp.float32(all_cells))
    adjoint = jnp.stack([res_re * norm_scale, res_im * norm_scale], axis=-1)
    adj_ext = padded_2(adjoint, (("slab", 0),), 1)
    lap_adj = laplace(adj_ext)
    grad_re = lap_adj[..., 0] + wave_sq * (eps_re * adjoint[..., 0] + eps_im * adjoint[..., 1])
    grad_im = lap_adj[..., 1] + wave_sq * (eps_re * adjoint[..., 1] - eps_im * adjoint[..., 0])
    grad_field = jnp.stack([grad_re, grad_im], axis=-1).reshape(cell_count, 2)
    d_hidden = jnp.dot(grad_field, head_proj.astype(jnp.float32).T, precision=lax.Precision.HIGHEST)
    sigma = jax.nn.sigmoid(preact)
    d_pre = (d_hidden * sigma * (1.0 + preact * (1.0 - sigma))).astype(jnp.bfloat16)
    grads = []
    for tap_index in range(27):
        grads.append(
            lax.dot_general(
                pieces[tap_index],
                d_pre,
                (((0,), (0,)), ((), ())),
                preferred_element_type=jnp.float32,
            )
        )
    grad = jnp.concatenate(grads, axis=0)
    scale = float(np.float32(1.0) / np.sqrt(np.float32(27 * channels)))
    new_master, new_moment, new_second, full = share_and_step(grad, master, moment, second, scale)
    new_kernel = full.reshape(kernel.shape)
    return (new_master, new_moment, new_second, new_kernel)


def solution(mesh):
    placed = (
        P("dp", "slab", None, None, None),
        P(),
        P(),
        P("dp", "slab", None, None),
        P("dp", "slab", None, None),
        P(),
        P(),
        P(("dp", "slab")),
        P(("dp", "slab")),
        P(("dp", "slab")),
    )
    return jax.shard_map(
        body,
        mesh=mesh,
        in_specs=placed,
        out_specs=(P(("dp", "slab")), P(("dp", "slab")), P(("dp", "slab")), P()),
        check_vma=False,
    )
```

```python
import functools

import jax
import jax.numpy as jnp
import numpy as np
from jax import lax
from jax.experimental import pallas as pl
from jax.experimental.pallas import tpu as pltpu
from jax.sharding import PartitionSpec as P

wave_sq = 0.3
beta_one = 0.9
beta_two = 0.99
learn_rate = 0.01
adam_eps = 1e-08


def spread(values, table, first):
    real = jnp.zeros(values.shape, jnp.float32)
    imag = jnp.zeros(values.shape, jnp.float32)
    for entry in range(table.shape[1]):
        hit = values == entry + first
        real = jnp.where(hit, table[0, entry], real)
        imag = jnp.where(hit, table[1, entry], imag)
    return real, imag


def grad_kernel(
    sizes,
    scale,
    norm_scale,
    features,
    weights,
    head,
    materials,
    ports,
    permittivity,
    port_source,
    grad,
    halo,
    near_taps,
    turned,
    factor,
    d_pad,
    edge_out,
    edge_in,
    send,
    recv,
):
    line, grid_w = sizes
    depth, cells, channels = features.shape
    wide = 3 * channels
    dp = lax.axis_index("dp")
    here = lax.axis_index("slab")
    has_low = here > 0
    has_high = here < line - 1
    low = (dp, here - 1)
    high = (dp, here + 1)

    def remote(source, target, stage, way, device):
        return pltpu.make_async_remote_copy(
            src_ref=source,
            dst_ref=target,
            send_sem=send.at[stage, way],
            recv_sem=recv.at[stage, way],
            device_id=device,
            device_id_type=pl.DeviceIdType.MESH,
        )

    def sends(stage):
        if stage == 0:
            return (
                remote(features.at[0], halo.at[1], 0, 1, low),
                remote(features.at[depth - 1], halo.at[0], 0, 0, high),
            )
        return (
            remote(edge_out.at[stage - 1, 0], edge_in.at[stage - 1, 1], stage, 1, low),
            remote(edge_out.at[stage - 1, 1], edge_in.at[stage - 1, 0], stage, 0, high),
        )

    def start(stage):
        to_low, to_high = sends(stage)
        pl.when(has_low)(to_low.start)
        pl.when(has_high)(to_high.start)

    def finish(stage):
        to_low, to_high = sends(stage)
        pl.when(has_low)(to_high.wait_recv)
        pl.when(has_high)(to_low.wait_recv)
        pl.when(has_low)(to_low.wait_send)
        pl.when(has_high)(to_high.wait_send)

    barrier = pltpu.get_barrier_semaphore()
    for there, device in ((has_low, low), (has_high, high)):

        @pl.when(there)
        def _(device=device):
            pl.semaphore_signal(
                barrier, inc=1, device_id=device, device_id_type=pl.DeviceIdType.MESH
            )

    pl.semaphore_wait(barrier, jnp.where(has_low, 1, 0) + jnp.where(has_high, 1, 0))

    start(0)
    for side, there in ((0, has_low), (1, has_high)):

        @pl.when(jnp.logical_not(there))
        def _(side=side):
            halo[side] = jnp.zeros((cells, channels), jnp.bfloat16)
            for stage in range(2):
                edge_in[stage, side] = jnp.zeros((8, cells), jnp.float32)

    empty = jnp.zeros((grid_w, wide), jnp.bfloat16)
    for plane in range(depth + 2):
        near_taps[plane, :grid_w] = empty
        near_taps[plane, grid_w + cells :] = empty
    for plane in range(depth):
        d_pad[plane, :grid_w] = empty[:, :channels]
        d_pad[plane, grid_w + cells :] = empty[:, :channels]

    column = lax.broadcasted_iota(jnp.int32, (cells, channels), 0) % grid_w

    def lay(plane, block):
        body_rows = pl.ds(grid_w, cells)
        values = block.astype(jnp.float32)
        before = jnp.where(column == 0, 0.0, pltpu.roll(values, 1, 0))
        after = jnp.where(column == grid_w - 1, 0.0, pltpu.roll(values, cells - 1, 0))
        near_taps[plane, body_rows, :channels] = before.astype(jnp.bfloat16)
        near_taps[plane, body_rows, channels : 2 * channels] = block
        near_taps[plane, body_rows, 2 * channels :] = after.astype(jnp.bfloat16)

    def taps(shift_z):
        total = None
        for shift_y in range(3):
            rows = near_taps[shift_z : shift_z + depth, shift_y * grid_w : shift_y * grid_w + cells]
            first = 9 * shift_z + 3 * shift_y
            part = jnp.dot(
                rows.reshape(depth * cells, wide),
                weights[first : first + 3].reshape(wide, channels),
                preferred_element_type=jnp.float32,
            )
            total = part if total is None else total + part
        return total

    def turn(plane):
        turned[:, plane * cells : (plane + 1) * cells] = near_taps[plane, grid_w : grid_w + cells].T

    for plane in range(depth):
        lay(plane + 1, features[plane])
    factor[...] = taps(1)
    finish(0)
    lay(0, halo[0])
    lay(depth + 1, halo[1])
    factor[...] += taps(0)
    preact = (factor[...] + taps(2)) * scale
    sigma = 1.0 / (1.0 + jnp.exp(-preact))
    hidden = (preact * sigma).astype(jnp.bfloat16)
    factor[...] = sigma * (1.0 + preact * (1.0 - sigma))
    field_rows = lax.dot_general(
        head[...], hidden, (((1,), (1,)), ((), ())), preferred_element_type=jnp.float32
    )[:8]
    field = [field_rows[:, plane * cells : (plane + 1) * cells] for plane in range(depth)]

    lane = lax.broadcasted_iota(jnp.int32, (8, cells), 1)
    row = lax.broadcasted_iota(jnp.int32, (8, cells), 0)
    lane_x = lane % grid_w

    def exchange(stage, planes):
        edge_out[stage - 1, 0] = planes[0]
        edge_out[stage - 1, 1] = planes[depth - 1]
        start(stage)

    def laplace(stage, planes):
        around = [edge_in[stage - 1, 0]] + planes + [edge_in[stage - 1, 1]]
        out = []
        for plane in range(depth):
            centre = planes[plane]
            near = around[plane] + around[plane + 2]
            near = near + jnp.where(lane < grid_w, 0.0, pltpu.roll(centre, grid_w, 1))
            near = near + jnp.where(
                lane >= cells - grid_w, 0.0, pltpu.roll(centre, cells - grid_w, 1)
            )
            near = near + jnp.where(lane_x == 0, 0.0, pltpu.roll(centre, 1, 1))
            near = near + jnp.where(lane_x == grid_w - 1, 0.0, pltpu.roll(centre, cells - 1, 1))
            out.append(near - 6.0 * centre)
        return out

    def both(real, imag):
        shape = (8, cells)
        imag = jnp.where(row == 1, jnp.broadcast_to(imag, shape), 0.0)
        return jnp.where(row == 0, jnp.broadcast_to(real, shape), imag)

    exchange(1, field)
    for plane in range(1, depth + 1):
        turn(plane)
    eps = [spread(materials[plane : plane + 1], permittivity, 0) for plane in range(depth)]
    src = [spread(ports[plane : plane + 1], port_source, 1) for plane in range(depth)]
    finish(1)
    adjoint = []
    for plane, lap in enumerate(laplace(1, field)):
        real, imag = field[plane][0:1], field[plane][1:2]
        eps_re, eps_im = eps[plane]
        src_re, src_im = src[plane]
        local = both(
            wave_sq * (eps_re * real - eps_im * imag) - src_re,
            wave_sq * (eps_re * imag + eps_im * real) - src_im,
        )
        adjoint.append((lap + local) * norm_scale)
    exchange(2, adjoint)
    turn(0)
    turn(depth + 1)
    finish(2)
    for plane, lap in enumerate(laplace(2, adjoint)):
        real, imag = adjoint[plane][0:1], adjoint[plane][1:2]
        eps_re, eps_im = eps[plane]
        back = lap + both(
            wave_sq * (eps_re * real + eps_im * imag), wave_sq * (eps_re * imag - eps_im * real)
        )
        columns = back.T
        projection = head[...].astype(jnp.float32)
        d_hidden = columns[:, 0:1] * projection[0:1] + columns[:, 1:2] * projection[1:2]
        d_pre = d_hidden * factor[plane * cells : (plane + 1) * cells]
        d_pad[plane, grid_w : grid_w + cells] = d_pre.astype(jnp.bfloat16)

    for shift_z in range(3):
        left = turned[:, shift_z * cells : (shift_z + depth) * cells]
        for shift_y in range(3):
            top = (2 - shift_y) * grid_w
            first = 9 * shift_z + 3 * shift_y
            grad[first : first + 3] = jnp.dot(
                left,
                d_pad[:, top : top + cells].reshape(depth * cells, channels),
                preferred_element_type=jnp.float32,
            ).reshape(3, channels, channels)


def local_grad(features, weights, head_proj, materials, ports, permittivity, port_source, scale):
    depth, grid_h, grid_w, channels = features.shape
    cells = grid_h * grid_w
    line = lax.axis_size("slab")
    all_cells = depth * cells * lax.axis_size("dp") * line
    norm_scale = float(np.float32(2.0) / np.sqrt(np.float32(all_cells)))
    vmem = pl.BlockSpec(memory_space=pltpu.VMEM)
    smem = pl.BlockSpec(memory_space=pltpu.SMEM)
    tall = cells + 2 * grid_w
    return pl.pallas_call(
        functools.partial(grad_kernel, (line, grid_w), scale, norm_scale),
        out_shape=jax.ShapeDtypeStruct((27, channels, channels), jnp.float32),
        in_specs=[vmem] * 5 + [smem] * 2,
        out_specs=vmem,
        scratch_shapes=[
            pltpu.VMEM((2, cells, channels), jnp.bfloat16),
            pltpu.VMEM((depth + 2, tall, 3 * channels), jnp.bfloat16),
            pltpu.VMEM((3 * channels, (depth + 2) * cells), jnp.bfloat16),
            pltpu.VMEM((depth * cells, channels), jnp.float32),
            pltpu.VMEM((depth, tall, channels), jnp.bfloat16),
            pltpu.VMEM((2, 2, 8, cells), jnp.float32),
            pltpu.VMEM((2, 2, 8, cells), jnp.float32),
            pltpu.SemaphoreType.DMA((3, 2)),
            pltpu.SemaphoreType.DMA((3, 2)),
        ],
        compiler_params=pltpu.CompilerParams(
            collective_id=1, has_side_effects=True, vmem_limit_bytes=48 * 1024 * 1024
        ),
    )(
        features.reshape(depth, cells, channels),
        weights,
        jnp.pad(head_proj.T, ((0, 14), (0, 0))),
        materials.reshape(depth, cells),
        ports.reshape(depth, cells),
        permittivity,
        port_source,
    )


def widen(block, rows):
    extra = rows - block.shape[0]
    if extra:
        block = jnp.concatenate([block, jnp.zeros((extra, block.shape[1]), block.dtype)], axis=0)
    return block.astype(jnp.bfloat16)


def share_kernel(
    scale,
    grad,
    master,
    moment,
    second,
    new_master,
    new_moment,
    new_second,
    full,
    pair_in,
    group_out,
    group_in,
    line_out,
    line_in,
    narrow,
    pair_send,
    pair_recv,
    group_send,
    group_recv,
    line_send,
    line_recv,
    line_back_send,
    line_back_recv,
    group_back_send,
    group_back_recv,
    pair_back_send,
    pair_back_recv,
):
    groups, _, line, rows, width = grad.shape
    padded = full.shape[3]
    dp = lax.axis_index("dp")
    here = lax.axis_index("slab")
    mine = dp // 2
    core = dp % 2
    sibling = (mine * 2 + 1 - core, here)

    def group_at(step):
        return (mine + step + groups) % groups

    def slab_at(step):
        return (here + step + line) % line

    def group_device(step):
        return (group_at(step) * 2 + core, here)

    def line_device(step):
        return (dp, slab_at(step))

    def remote(source, target, send, recv, device):
        return pltpu.make_async_remote_copy(
            src_ref=source,
            dst_ref=target,
            send_sem=send,
            recv_sem=recv,
            device_id=device,
            device_id_type=pl.DeviceIdType.MESH,
        )

    def pair_copy(k):
        return remote(
            grad.at[group_at(k), 1 - core], pair_in.at[k], pair_send.at[k], pair_recv.at[k], sibling
        )

    def group_copy(k, j):
        return remote(
            group_out.at[k - 1, j],
            group_in.at[k - 1, j],
            group_send.at[k - 1, j],
            group_recv.at[k - 1, j],
            group_device(k),
        )

    def line_copy(j):
        return remote(
            line_out.at[j - 1], line_in.at[j - 1], line_send.at[j - 1], line_recv.at[j - 1], line_device(j)
        )

    def line_back(j):
        spot = full.at[mine, core, here]
        return remote(spot, spot, line_back_send.at[j - 1], line_back_recv.at[j - 1], line_device(j))

    def group_back(k, j):
        spot = full.at[mine, core, slab_at(-j)]
        return remote(
            spot, spot, group_back_send.at[k - 1, j], group_back_recv.at[k - 1, j], group_device(k)
        )

    def pair_back(k, j):
        spot = full.at[group_at(-k), core, slab_at(-j)]
        return remote(spot, spot, pair_back_send.at[k, j], pair_back_recv.at[k, j], sibling)

    others = [sibling]
    others += [group_device(k) for k in range(1, groups)]
    others += [line_device(j) for j in range(1, line)]
    barrier = pltpu.get_barrier_semaphore()
    for device in others:
        pl.semaphore_signal(barrier, inc=1, device_id=device, device_id_type=pl.DeviceIdType.MESH)
    pl.semaphore_wait(barrier, len(others))

    group_order = list(range(1, groups)) + [0]
    line_order = list(range(1, line)) + [0]
    for k in group_order:
        pair_copy(k).start()
    for k in group_order[:-1]:
        pair_copy(k).wait_recv()
        for j in line_order:
            slab = slab_at(j)
            group_out[k - 1, j] = widen(grad[group_at(k), core, slab] + pair_in[k, slab], padded)
            group_copy(k, j).start()
    pair_copy(0).wait_recv()
    total = None
    for j in line_order:
        slab = slab_at(j)
        total = grad[mine, core, slab] + pair_in[0, slab]
        for k in range(1, groups):
            group_copy(k, j).wait_recv()
            total = total + group_in[k - 1, j].astype(jnp.float32)[:rows]
        if j:
            line_out[j - 1] = widen(total, padded)
            line_copy(j).start()
    for j in range(1, line):
        line_copy(j).wait_recv()
        total = total + line_in[j - 1].astype(jnp.float32)[:rows]

    total = total * scale
    parts = width // 128
    for part in range(parts):
        narrow[pl.ds(part, rows, stride=parts), :] = total[:, part * 128 : part * 128 + 128]
    share = narrow[...]
    stepped = beta_one * moment[...] + (1.0 - beta_one) * share
    squared = beta_two * second[...] + (1.0 - beta_two) * share * share
    updated = master[...] - learn_rate * stepped / (jnp.sqrt(squared) + adam_eps)
    new_moment[...] = stepped
    new_second[...] = squared
    new_master[...] = updated
    narrow[...] = updated
    block = jnp.concatenate(
        [narrow[pl.ds(part, rows, stride=parts), :] for part in range(parts)], axis=1
    )
    full[mine, core, here] = widen(block, padded)

    for j in range(1, line):
        line_back(j).start()
    for k in range(1, groups):
        group_back(k, 0).start()
    pair_back(0, 0).start()
    for j in range(1, line):
        line_back(j).wait_recv()
        for k in range(1, groups):
            group_back(k, j).start()
        pair_back(0, j).start()
    for j in range(line):
        for k in range(1, groups):
            group_back(k, j).wait_recv()
            pair_back(k, j).start()
    for j in range(line):
        for k in range(groups):
            pair_back(k, j).wait_recv()
    for k in range(groups):
        pair_copy(k).wait_send()
        for j in range(line):
            pair_back(k, j).wait_send()
            if k:
                group_copy(k, j).wait_send()
                group_back(k, j).wait_send()
    for j in range(1, line):
        line_copy(j).wait_send()
        line_back(j).wait_send()


def share_and_step(grad, master, moment, second, scale):
    rows_all, width = grad.shape
    groups = lax.axis_size("dp") // 2
    line = lax.axis_size("slab")
    rows = rows_all // (groups * 2 * line)
    padded = -(-rows // 16) * 16
    flat = (master.size // 128, 128)
    vmem = pl.BlockSpec(memory_space=pltpu.VMEM)
    dma = pltpu.SemaphoreType.DMA
    state = jax.ShapeDtypeStruct(flat, jnp.float32)
    out = pl.pallas_call(
        functools.partial(share_kernel, scale),
        out_shape=[
            state,
            state,
            state,
            jax.ShapeDtypeStruct((groups, 2, line, padded, width), jnp.bfloat16),
        ],
        in_specs=[vmem] * 4,
        out_specs=[vmem] * 4,
        scratch_shapes=[
            pltpu.VMEM((groups, line, rows, width), jnp.float32),
            pltpu.VMEM((groups - 1, line, padded, width), jnp.bfloat16),
            pltpu.VMEM((groups - 1, line, padded, width), jnp.bfloat16),
            pltpu.VMEM((line - 1, padded, width), jnp.bfloat16),
            pltpu.VMEM((line - 1, padded, width), jnp.bfloat16),
            pltpu.VMEM(flat, jnp.float32),
            dma((groups,)),
            dma((groups,)),
            dma((groups - 1, line)),
            dma((groups - 1, line)),
            dma((line - 1,)),
            dma((line - 1,)),
            dma((line - 1,)),
            dma((line - 1,)),
            dma((groups - 1, line)),
            dma((groups - 1, line)),
            dma((groups, line)),
            dma((groups, line)),
        ],
        compiler_params=pltpu.CompilerParams(
            collective_id=0, has_side_effects=True, vmem_limit_bytes=48 * 1024 * 1024
        ),
    )(
        grad.reshape(groups, 2, line, rows, width),
        master.reshape(flat),
        moment.reshape(flat),
        second.reshape(flat),
    )
    full = out[3][:, :, :, :rows].reshape(rows_all, width)
    return [part.reshape(-1) for part in out[:3]] + [full]


def body(
    features,
    kernel,
    head_proj,
    material_ids,
    port_ids,
    permittivity,
    port_source,
    master,
    moment,
    second,
):
    channels = features.shape[-1]
    scale = float(np.float32(1.0) / np.sqrt(np.float32(27 * channels)))
    grad = local_grad(
        features[0],
        kernel,
        head_proj,
        material_ids[0],
        port_ids[0],
        permittivity,
        port_source,
        scale,
    ).reshape(27 * channels, channels)
    new_master, new_moment, new_second, full = share_and_step(grad, master, moment, second, scale)
    new_kernel = full.reshape(kernel.shape)
    return (new_master, new_moment, new_second, new_kernel)


def solution(mesh):
    placed = (
        P("dp", "slab", None, None, None),
        P(),
        P(),
        P("dp", "slab", None, None),
        P("dp", "slab", None, None),
        P(),
        P(),
        P(("dp", "slab")),
        P(("dp", "slab")),
        P(("dp", "slab")),
    )
    return jax.shard_map(
        body,
        mesh=mesh,
        in_specs=placed,
        out_specs=(P(("dp", "slab")), P(("dp", "slab")), P(("dp", "slab")), P()),
        check_vma=False,
    )
```

```python
import functools

import jax
import jax.numpy as jnp
import numpy as np
from jax import lax
from jax.experimental import pallas as pl
from jax.experimental.pallas import tpu as pltpu
from jax.sharding import PartitionSpec as P

wave_sq = 0.3
beta_one = 0.9
beta_two = 0.99
learn_rate = 0.01
adam_eps = 1e-08


def spread(values, table, first):
    real = jnp.zeros(values.shape, jnp.float32)
    imag = jnp.zeros(values.shape, jnp.float32)
    for entry in range(table.shape[1]):
        hit = values == entry + first
        real = jnp.where(hit, table[0, entry], real)
        imag = jnp.where(hit, table[1, entry], imag)
    return real, imag


def widen(block, rows):
    extra = rows - block.shape[0]
    if extra:
        block = jnp.concatenate([block, jnp.zeros((extra, block.shape[1]), block.dtype)], axis=0)
    return block.astype(jnp.bfloat16)


def step_kernel(
    sizes,
    scale,
    norm_scale,
    features,
    weights_far,
    head,
    materials,
    ports,
    permittivity,
    port_source,
    master,
    moment,
    second,
    new_master,
    new_moment,
    new_second,
    full,
    grad,
    blocks,
    weights,
    halo,
    near_taps,
    turned,
    factor,
    d_pad,
    edge_out,
    edge_in,
    pair_in,
    group_out,
    group_in,
    line_out,
    line_in,
    narrow,
    weight_sem,
    send,
    recv,
    pair_send,
    pair_recv,
    group_send,
    group_recv,
    line_send,
    line_recv,
    line_back_send,
    line_back_recv,
    group_back_send,
    group_back_recv,
    pair_back_send,
    pair_back_recv,
):
    line, grid_w = sizes
    depth, cells, channels = features.shape
    groups, _, _, padded, width = full.shape
    rows = grad.shape[0] // (groups * 2 * line)
    wide = 3 * channels
    dp = lax.axis_index("dp")
    here = lax.axis_index("slab")
    mine = dp // 2
    core = dp % 2
    sibling = (mine * 2 + 1 - core, here)

    def group_at(step):
        return (mine + step + groups) % groups

    def slab_at(step):
        return (here + step + line) % line

    def group_device(step):
        return (group_at(step) * 2 + core, here)

    def line_device(step):
        return (dp, slab_at(step))

    has_low = here > 0
    has_high = here < line - 1
    low = (dp, here - 1)
    high = (dp, here + 1)

    def remote(source, target, stage, way, device):
        return pltpu.make_async_remote_copy(
            src_ref=source,
            dst_ref=target,
            send_sem=send.at[stage, way],
            recv_sem=recv.at[stage, way],
            device_id=device,
            device_id_type=pl.DeviceIdType.MESH,
        )

    def sends(stage):
        if stage == 0:
            return (
                remote(features.at[0], halo.at[1], 0, 1, low),
                remote(features.at[depth - 1], halo.at[0], 0, 0, high),
            )
        return (
            remote(edge_out.at[stage - 1, 0], edge_in.at[stage - 1, 1], stage, 1, low),
            remote(edge_out.at[stage - 1, 1], edge_in.at[stage - 1, 0], stage, 0, high),
        )

    def start(stage):
        to_low, to_high = sends(stage)
        pl.when(has_low)(to_low.start)
        pl.when(has_high)(to_high.start)

    def finish(stage):
        to_low, to_high = sends(stage)
        pl.when(has_low)(to_high.wait_recv)
        pl.when(has_high)(to_low.wait_recv)
        pl.when(has_low)(to_low.wait_send)
        pl.when(has_high)(to_high.wait_send)

    def remote_pair(source, target, send_sem, recv_sem, device):
        return pltpu.make_async_remote_copy(
            src_ref=source,
            dst_ref=target,
            send_sem=send_sem,
            recv_sem=recv_sem,
            device_id=device,
            device_id_type=pl.DeviceIdType.MESH,
        )

    def block_rows(group, side, slab):
        first = ((group * 2 + side) * line + slab) * rows
        return pl.ds(pl.multiple_of(first, 8), rows)

    def block_at(group, side, slab):
        if rows % 8:
            return blocks.at[(group * 2 + side) * line + slab]
        return grad.at[block_rows(group, side, slab)]

    def pair_copy(group, slab):
        return remote_pair(
            block_at(group, 1 - core, slab),
            pair_in.at[group, slab],
            pair_send.at[group, slab],
            pair_recv.at[group, slab],
            sibling,
        )

    def pair_sum(group, slab):
        pair_copy(group, slab).wait_recv()
        return block_at(group, core, slab)[...] + pair_in[group, slab]

    def group_copy(k, j):
        return remote_pair(
            group_out.at[k - 1, j],
            group_in.at[k - 1, j],
            group_send.at[k - 1, j],
            group_recv.at[k - 1, j],
            group_device(k),
        )

    def line_copy(j):
        return remote_pair(
            line_out.at[j - 1], line_in.at[j - 1], line_send.at[j - 1], line_recv.at[j - 1], line_device(j)
        )

    def line_back(j):
        spot = full.at[mine, core, here]
        return remote_pair(spot, spot, line_back_send.at[j - 1], line_back_recv.at[j - 1], line_device(j))

    def group_back(k, j):
        spot = full.at[mine, core, slab_at(-j)]
        return remote_pair(
            spot, spot, group_back_send.at[k - 1, j], group_back_recv.at[k - 1, j], group_device(k)
        )

    def pair_back(k, j):
        spot = full.at[group_at(-k), core, slab_at(-j)]
        return remote_pair(spot, spot, pair_back_send.at[k, j], pair_back_recv.at[k, j], sibling)

    weight_copy = pltpu.make_async_copy(weights_far, weights, weight_sem)
    weight_copy.start()
    others = [sibling]
    others += [group_device(k) for k in range(1, groups)]
    others += [line_device(j) for j in range(1, line)]
    barrier = pltpu.get_barrier_semaphore()
    for device in others:
        pl.semaphore_signal(barrier, inc=1, device_id=device, device_id_type=pl.DeviceIdType.MESH)
    pl.semaphore_wait(barrier, len(others))

    start(0)
    for side, there in ((0, has_low), (1, has_high)):

        @pl.when(jnp.logical_not(there))
        def _(side=side):
            halo[side] = jnp.zeros((cells, channels), jnp.bfloat16)
            for stage in range(2):
                edge_in[stage, side] = jnp.zeros((8, cells), jnp.float32)

    empty = jnp.zeros((grid_w, wide), jnp.bfloat16)
    for plane in range(depth + 2):
        near_taps[plane, :grid_w] = empty
        near_taps[plane, grid_w + cells :] = empty
    for plane in range(depth):
        d_pad[plane, :grid_w] = empty[:, :channels]
        d_pad[plane, grid_w + cells :] = empty[:, :channels]

    column = lax.broadcasted_iota(jnp.int32, (cells, channels), 0) % grid_w

    def lay(plane, block):
        body_rows = pl.ds(grid_w, cells)
        values = block.astype(jnp.float32)
        before = jnp.where(column == 0, 0.0, pltpu.roll(values, 1, 0))
        after = jnp.where(column == grid_w - 1, 0.0, pltpu.roll(values, cells - 1, 0))
        near_taps[plane, body_rows, :channels] = before.astype(jnp.bfloat16)
        near_taps[plane, body_rows, channels : 2 * channels] = block
        near_taps[plane, body_rows, 2 * channels :] = after.astype(jnp.bfloat16)

    def taps(shift_z):
        total = None
        for shift_y in range(3):
            rows = near_taps[shift_z : shift_z + depth, shift_y * grid_w : shift_y * grid_w + cells]
            first = 9 * shift_z + 3 * shift_y
            part = jnp.dot(
                rows.reshape(depth * cells, wide),
                weights[first : first + 3].reshape(wide, channels),
                preferred_element_type=jnp.float32,
            )
            total = part if total is None else total + part
        return total

    def turn(plane):
        turned[:, plane * cells : (plane + 1) * cells] = near_taps[plane, grid_w : grid_w + cells].T

    for plane in range(depth):
        lay(plane + 1, features[plane])
    weight_copy.wait()
    factor[...] = taps(1)
    finish(0)
    lay(0, halo[0])
    lay(depth + 1, halo[1])
    factor[...] += taps(0)
    preact = (factor[...] + taps(2)) * scale
    sigma = 1.0 / (1.0 + jnp.exp(-preact))
    hidden = (preact * sigma).astype(jnp.bfloat16)
    factor[...] = sigma * (1.0 + preact * (1.0 - sigma))
    field_rows = lax.dot_general(
        head[...], hidden, (((1,), (1,)), ((), ())), preferred_element_type=jnp.float32
    )[:8]
    field = [field_rows[:, plane * cells : (plane + 1) * cells] for plane in range(depth)]

    lane = lax.broadcasted_iota(jnp.int32, (8, cells), 1)
    row = lax.broadcasted_iota(jnp.int32, (8, cells), 0)
    lane_x = lane % grid_w

    def exchange(stage, planes):
        edge_out[stage - 1, 0] = planes[0]
        edge_out[stage - 1, 1] = planes[depth - 1]
        start(stage)

    def laplace(stage, planes):
        around = [edge_in[stage - 1, 0]] + planes + [edge_in[stage - 1, 1]]
        out = []
        for plane in range(depth):
            centre = planes[plane]
            near = around[plane] + around[plane + 2]
            near = near + jnp.where(lane < grid_w, 0.0, pltpu.roll(centre, grid_w, 1))
            near = near + jnp.where(
                lane >= cells - grid_w, 0.0, pltpu.roll(centre, cells - grid_w, 1)
            )
            near = near + jnp.where(lane_x == 0, 0.0, pltpu.roll(centre, 1, 1))
            near = near + jnp.where(lane_x == grid_w - 1, 0.0, pltpu.roll(centre, cells - 1, 1))
            out.append(near - 6.0 * centre)
        return out

    def both(real, imag):
        shape = (8, cells)
        imag = jnp.where(row == 1, jnp.broadcast_to(imag, shape), 0.0)
        return jnp.where(row == 0, jnp.broadcast_to(real, shape), imag)

    exchange(1, field)
    for plane in range(1, depth + 1):
        turn(plane)
    eps = [spread(materials[plane : plane + 1], permittivity, 0) for plane in range(depth)]
    src = [spread(ports[plane : plane + 1], port_source, 1) for plane in range(depth)]
    finish(1)
    adjoint = []
    for plane, lap in enumerate(laplace(1, field)):
        real, imag = field[plane][0:1], field[plane][1:2]
        eps_re, eps_im = eps[plane]
        src_re, src_im = src[plane]
        local = both(
            wave_sq * (eps_re * real - eps_im * imag) - src_re,
            wave_sq * (eps_re * imag + eps_im * real) - src_im,
        )
        adjoint.append((lap + local) * norm_scale)
    exchange(2, adjoint)
    turn(0)
    turn(depth + 1)
    finish(2)
    for plane, lap in enumerate(laplace(2, adjoint)):
        real, imag = adjoint[plane][0:1], adjoint[plane][1:2]
        eps_re, eps_im = eps[plane]
        back = lap + both(
            wave_sq * (eps_re * real + eps_im * imag), wave_sq * (eps_re * imag - eps_im * real)
        )
        columns = back.T
        projection = head[...].astype(jnp.float32)
        d_hidden = columns[:, 0:1] * projection[0:1] + columns[:, 1:2] * projection[1:2]
        d_pre = d_hidden * factor[plane * cells : (plane + 1) * cells]
        d_pad[plane, grid_w : grid_w + cells] = d_pre.astype(jnp.bfloat16)

    ready = 0
    group_rows = 2 * line * rows
    for shift_z in range(3):
        left = turned[:, shift_z * cells : (shift_z + depth) * cells]
        for shift_y in range(3):
            top = (2 - shift_y) * grid_w
            first = 9 * shift_z + 3 * shift_y
            first = first * channels
            grad[first : first + wide] = jnp.dot(
                left,
                d_pad[:, top : top + cells].reshape(depth * cells, channels),
                preferred_element_type=jnp.float32,
            )
            while rows % 8 == 0 and ready < groups and (ready + 1) * group_rows <= first + wide:
                for slab in range(line):
                    pair_copy(ready, slab).start()
                ready += 1
    if rows % 8:
        for spot in range(groups * 2 * line):
            blocks[spot] = grad[spot * rows : (spot + 1) * rows]
        for group in range(groups):
            for slab in range(line):
                pair_copy(group, slab).start()

    group_order = list(range(1, groups)) + [0]
    line_order = list(range(1, line)) + [0]
    for k in group_order[:-1]:
        for j in line_order:
            slab = slab_at(j)
            group_out[k - 1, j] = widen(pair_sum(group_at(k), slab), padded)
            group_copy(k, j).start()
    total = None
    for j in line_order:
        slab = slab_at(j)
        total = pair_sum(mine, slab)
        for k in range(1, groups):
            group_copy(k, j).wait_recv()
            total = total + group_in[k - 1, j].astype(jnp.float32)[:rows]
        if j:
            line_out[j - 1] = widen(total, padded)
            line_copy(j).start()
    for j in range(1, line):
        line_copy(j).wait_recv()
        total = total + line_in[j - 1].astype(jnp.float32)[:rows]

    total = total * scale
    parts = width // 128
    for part in range(parts):
        narrow[pl.ds(part, rows, stride=parts), :] = total[:, part * 128 : part * 128 + 128]
    share = narrow[...]
    stepped = beta_one * moment[...] + (1.0 - beta_one) * share
    squared = beta_two * second[...] + (1.0 - beta_two) * share * share
    updated = master[...] - learn_rate * stepped / (jnp.sqrt(squared) + adam_eps)
    new_moment[...] = stepped
    new_second[...] = squared
    new_master[...] = updated
    narrow[...] = updated
    block = jnp.concatenate(
        [narrow[pl.ds(part, rows, stride=parts), :] for part in range(parts)], axis=1
    )
    full[mine, core, here] = widen(block, padded)

    for j in range(1, line):
        line_back(j).start()
    for k in range(1, groups):
        group_back(k, 0).start()
    pair_back(0, 0).start()
    for j in range(1, line):
        line_back(j).wait_recv()
        for k in range(1, groups):
            group_back(k, j).start()
        pair_back(0, j).start()
    for j in range(line):
        for k in range(1, groups):
            group_back(k, j).wait_recv()
            pair_back(k, j).start()
    for j in range(line):
        for k in range(groups):
            pair_back(k, j).wait_recv()
    for k in range(groups):
        for j in range(line):
            pair_copy(k, j).wait_send()
            pair_back(k, j).wait_send()
            if k:
                group_copy(k, j).wait_send()
                group_back(k, j).wait_send()
    for j in range(1, line):
        line_copy(j).wait_send()
        line_back(j).wait_send()


def whole_step(features, weights, head_proj, codes, tables, states):
    depth, grid_h, grid_w, channels = features.shape
    cells = grid_h * grid_w
    line = lax.axis_size("slab")
    groups = lax.axis_size("dp") // 2
    all_cells = depth * cells * groups * 2 * line
    scale = float(np.float32(1.0) / np.sqrt(np.float32(27 * channels)))
    norm_scale = float(np.float32(2.0) / np.sqrt(np.float32(all_cells)))
    rows_all = 27 * channels
    rows = rows_all // (groups * 2 * line)
    padded = -(-rows // 16) * 16
    flat = (rows * channels // 128, 128)
    tall = cells + 2 * grid_w
    spare = (groups * 2 * line, rows, channels) if rows % 8 else (1, 8, 128)
    vmem = pl.BlockSpec(memory_space=pltpu.VMEM)
    smem = pl.BlockSpec(memory_space=pltpu.SMEM)
    dma = pltpu.SemaphoreType.DMA
    state = jax.ShapeDtypeStruct(flat, jnp.float32)
    out = pl.pallas_call(
        functools.partial(step_kernel, (line, grid_w), scale, norm_scale),
        out_shape=[
            state,
            state,
            state,
            jax.ShapeDtypeStruct((groups, 2, line, padded, channels), jnp.bfloat16),
        ],
        in_specs=[vmem, pl.BlockSpec(memory_space=pl.ANY)] + [vmem] * 3 + [smem] * 2 + [vmem] * 3,
        out_specs=[vmem] * 4,
        scratch_shapes=[
            pltpu.VMEM((rows_all, channels), jnp.float32),
            pltpu.VMEM(spare, jnp.float32),
            pltpu.VMEM((27, channels, channels), jnp.bfloat16),
            pltpu.VMEM((2, cells, channels), jnp.bfloat16),
            pltpu.VMEM((depth + 2, tall, 3 * channels), jnp.bfloat16),
            pltpu.VMEM((3 * channels, (depth + 2) * cells), jnp.bfloat16),
            pltpu.VMEM((depth * cells, channels), jnp.float32),
            pltpu.VMEM((depth, tall, channels), jnp.bfloat16),
            pltpu.VMEM((2, 2, 8, cells), jnp.float32),
            pltpu.VMEM((2, 2, 8, cells), jnp.float32),
            pltpu.VMEM((groups, line, rows, channels), jnp.float32),
            pltpu.VMEM((groups - 1, line, padded, channels), jnp.bfloat16),
            pltpu.VMEM((groups - 1, line, padded, channels), jnp.bfloat16),
            pltpu.VMEM((line - 1, padded, channels), jnp.bfloat16),
            pltpu.VMEM((line - 1, padded, channels), jnp.bfloat16),
            pltpu.VMEM(flat, jnp.float32),
            dma,
            dma((3, 2)),
            dma((3, 2)),
            dma((groups, line)),
            dma((groups, line)),
            dma((groups - 1, line)),
            dma((groups - 1, line)),
            dma((line - 1,)),
            dma((line - 1,)),
            dma((line - 1,)),
            dma((line - 1,)),
            dma((groups - 1, line)),
            dma((groups - 1, line)),
            dma((groups, line)),
            dma((groups, line)),
        ],
        compiler_params=pltpu.CompilerParams(
            collective_id=0, has_side_effects=True, vmem_limit_bytes=58 * 1024 * 1024
        ),
    )(
        features.reshape(depth, cells, channels),
        weights,
        jnp.pad(head_proj.T, ((0, 14), (0, 0))),
        *[part.reshape(depth, cells) for part in codes],
        *tables,
        *[part.reshape(flat) for part in states],
    )
    full = out[3][:, :, :, :rows].reshape(weights.shape)
    return tuple(part.reshape(-1) for part in out[:3]) + (full,)


def body(
    features,
    kernel,
    head_proj,
    material_ids,
    port_ids,
    permittivity,
    port_source,
    master,
    moment,
    second,
):
    return whole_step(
        features[0],
        kernel,
        head_proj,
        (material_ids[0], port_ids[0]),
        (permittivity, port_source),
        (master, moment, second),
    )


def solution(mesh):
    placed = (
        P("dp", "slab", None, None, None),
        P(),
        P(),
        P("dp", "slab", None, None),
        P("dp", "slab", None, None),
        P(),
        P(),
        P(("dp", "slab")),
        P(("dp", "slab")),
        P(("dp", "slab")),
    )
    return jax.shard_map(
        body,
        mesh=mesh,
        in_specs=placed,
        out_specs=(P(("dp", "slab")), P(("dp", "slab")), P(("dp", "slab")), P()),
        check_vma=False,
    )
```

```python
import functools

import jax
import jax.numpy as jnp
import numpy as np
from jax import lax
from jax.experimental import pallas as pl
from jax.experimental.pallas import tpu as pltpu
from jax.sharding import PartitionSpec as P

wave_sq = 0.3
beta_one = 0.9
beta_two = 0.99
learn_rate = 0.01
adam_eps = 1e-08


def spread(values, table, first):
    real = jnp.zeros(values.shape, jnp.float32)
    imag = jnp.zeros(values.shape, jnp.float32)
    for entry in range(table.shape[1]):
        hit = values == entry + first
        real = jnp.where(hit, table[0, entry], real)
        imag = jnp.where(hit, table[1, entry], imag)
    return real, imag


def widen(block, rows):
    extra = rows - block.shape[0]
    if extra:
        block = jnp.concatenate([block, jnp.zeros((extra, block.shape[1]), block.dtype)], axis=0)
    return block.astype(jnp.bfloat16)


def step_kernel(
    sizes,
    scale,
    norm_scale,
    features,
    weights,
    head,
    materials,
    ports,
    permittivity,
    port_source,
    master,
    moment,
    second,
    new_master,
    new_moment,
    new_second,
    full,
    grad,
    blocks,
    halo,
    near_taps,
    turned,
    factor,
    d_pad,
    edge_out,
    edge_in,
    pair_in,
    group_out,
    group_in,
    line_out,
    line_in,
    narrow,
    send,
    recv,
    pair_send,
    pair_recv,
    group_send,
    group_recv,
    line_send,
    line_recv,
    line_back_send,
    line_back_recv,
    group_back_send,
    group_back_recv,
    pair_back_send,
    pair_back_recv,
):
    line, grid_w = sizes
    depth, cells, channels = features.shape
    groups, _, _, padded, width = full.shape
    rows = grad.shape[0] // (groups * 2 * line)
    wide = 3 * channels
    dp = lax.axis_index("dp")
    here = lax.axis_index("slab")
    mine = dp // 2
    core = dp % 2
    sibling = (mine * 2 + 1 - core, here)

    def group_at(step):
        return (mine + step + groups) % groups

    def slab_at(step):
        return (here + step + line) % line

    def group_device(step):
        return (group_at(step) * 2 + core, here)

    def line_device(step):
        return (dp, slab_at(step))

    has_low = here > 0
    has_high = here < line - 1
    low = (dp, here - 1)
    high = (dp, here + 1)

    def remote(source, target, stage, way, device):
        return pltpu.make_async_remote_copy(
            src_ref=source,
            dst_ref=target,
            send_sem=send.at[stage, way],
            recv_sem=recv.at[stage, way],
            device_id=device,
            device_id_type=pl.DeviceIdType.MESH,
        )

    def sends(stage):
        if stage == 0:
            return (
                remote(features.at[0], halo.at[1], 0, 1, low),
                remote(features.at[depth - 1], halo.at[0], 0, 0, high),
            )
        return (
            remote(edge_out.at[stage - 1, 0], edge_in.at[stage - 1, 1], stage, 1, low),
            remote(edge_out.at[stage - 1, 1], edge_in.at[stage - 1, 0], stage, 0, high),
        )

    def start(stage):
        to_low, to_high = sends(stage)
        pl.when(has_low)(to_low.start)
        pl.when(has_high)(to_high.start)

    def finish(stage):
        to_low, to_high = sends(stage)
        pl.when(has_low)(to_high.wait_recv)
        pl.when(has_high)(to_low.wait_recv)
        pl.when(has_low)(to_low.wait_send)
        pl.when(has_high)(to_high.wait_send)

    def remote_pair(source, target, send_sem, recv_sem, device):
        return pltpu.make_async_remote_copy(
            src_ref=source,
            dst_ref=target,
            send_sem=send_sem,
            recv_sem=recv_sem,
            device_id=device,
            device_id_type=pl.DeviceIdType.MESH,
        )

    def block_rows(group, side, slab):
        first = ((group * 2 + side) * line + slab) * rows
        return pl.ds(pl.multiple_of(first, 8), rows)

    def block_at(group, side, slab):
        if rows % 8:
            return blocks.at[(group * 2 + side) * line + slab]
        return grad.at[block_rows(group, side, slab)]

    def pair_copy(group, slab):
        return remote_pair(
            block_at(group, 1 - core, slab),
            pair_in.at[group, slab],
            pair_send.at[group, slab],
            pair_recv.at[group, slab],
            sibling,
        )

    def pair_sum(group, slab):
        pair_copy(group, slab).wait_recv()
        return block_at(group, core, slab)[...] + pair_in[group, slab]

    def group_copy(k, j):
        return remote_pair(
            group_out.at[k - 1, j],
            group_in.at[k - 1, j],
            group_send.at[k - 1, j],
            group_recv.at[k - 1, j],
            group_device(k),
        )

    def line_copy(j):
        return remote_pair(
            line_out.at[j - 1], line_in.at[j - 1], line_send.at[j - 1], line_recv.at[j - 1], line_device(j)
        )

    def line_back(j):
        spot = full.at[mine, core, here]
        return remote_pair(spot, spot, line_back_send.at[j - 1], line_back_recv.at[j - 1], line_device(j))

    def group_back(k, j):
        spot = full.at[mine, core, slab_at(-j)]
        return remote_pair(
            spot, spot, group_back_send.at[k - 1, j], group_back_recv.at[k - 1, j], group_device(k)
        )

    def pair_back(k, j):
        spot = full.at[group_at(-k), core, slab_at(-j)]
        return remote_pair(spot, spot, pair_back_send.at[k, j], pair_back_recv.at[k, j], sibling)

    others = [sibling]
    others += [group_device(k) for k in range(1, groups)]
    others += [line_device(j) for j in range(1, line)]
    barrier = pltpu.get_barrier_semaphore()
    for device in others:
        pl.semaphore_signal(barrier, inc=1, device_id=device, device_id_type=pl.DeviceIdType.MESH)
    pl.semaphore_wait(barrier, len(others))

    start(0)
    for side, there in ((0, has_low), (1, has_high)):

        @pl.when(jnp.logical_not(there))
        def _(side=side):
            halo[side] = jnp.zeros((cells, channels), jnp.bfloat16)
            for stage in range(2):
                edge_in[stage, side] = jnp.zeros((8, cells), jnp.float32)

    empty = jnp.zeros((grid_w, wide), jnp.bfloat16)
    for plane in range(depth + 2):
        near_taps[plane, :grid_w] = empty
        near_taps[plane, grid_w + cells :] = empty
    for plane in range(depth):
        d_pad[plane, :grid_w] = empty[:, :channels]
        d_pad[plane, grid_w + cells :] = empty[:, :channels]

    column = lax.broadcasted_iota(jnp.int32, (cells, channels), 0) % grid_w

    def lay(plane, block):
        body_rows = pl.ds(grid_w, cells)
        values = block.astype(jnp.float32)
        before = jnp.where(column == 0, 0.0, pltpu.roll(values, 1, 0))
        after = jnp.where(column == grid_w - 1, 0.0, pltpu.roll(values, cells - 1, 0))
        near_taps[plane, body_rows, :channels] = before.astype(jnp.bfloat16)
        near_taps[plane, body_rows, channels : 2 * channels] = block
        near_taps[plane, body_rows, 2 * channels :] = after.astype(jnp.bfloat16)

    def taps(shift_z):
        total = None
        for shift_y in range(3):
            rows = near_taps[shift_z : shift_z + depth, shift_y * grid_w : shift_y * grid_w + cells]
            first = 9 * shift_z + 3 * shift_y
            part = jnp.dot(
                rows.reshape(depth * cells, wide),
                weights[first : first + 3].reshape(wide, channels),
                preferred_element_type=jnp.float32,
            )
            total = part if total is None else total + part
        return total

    def turn(plane):
        turned[:, plane * cells : (plane + 1) * cells] = near_taps[plane, grid_w : grid_w + cells].T

    for plane in range(depth):
        lay(plane + 1, features[plane])
    factor[...] = taps(1)
    finish(0)
    lay(0, halo[0])
    lay(depth + 1, halo[1])
    factor[...] += taps(0)
    preact = (factor[...] + taps(2)) * scale
    sigma = 1.0 / (1.0 + jnp.exp(-preact))
    hidden = (preact * sigma).astype(jnp.bfloat16)
    factor[...] = sigma * (1.0 + preact * (1.0 - sigma))
    field_rows = lax.dot_general(
        head[...], hidden, (((1,), (1,)), ((), ())), preferred_element_type=jnp.float32
    )[:8]
    field = [field_rows[:, plane * cells : (plane + 1) * cells] for plane in range(depth)]

    lane = lax.broadcasted_iota(jnp.int32, (8, cells), 1)
    row = lax.broadcasted_iota(jnp.int32, (8, cells), 0)
    lane_x = lane % grid_w

    def exchange(stage, planes):
        edge_out[stage - 1, 0] = planes[0]
        edge_out[stage - 1, 1] = planes[depth - 1]
        start(stage)

    def laplace(stage, planes):
        around = [edge_in[stage - 1, 0]] + planes + [edge_in[stage - 1, 1]]
        out = []
        for plane in range(depth):
            centre = planes[plane]
            near = around[plane] + around[plane + 2]
            near = near + jnp.where(lane < grid_w, 0.0, pltpu.roll(centre, grid_w, 1))
            near = near + jnp.where(
                lane >= cells - grid_w, 0.0, pltpu.roll(centre, cells - grid_w, 1)
            )
            near = near + jnp.where(lane_x == 0, 0.0, pltpu.roll(centre, 1, 1))
            near = near + jnp.where(lane_x == grid_w - 1, 0.0, pltpu.roll(centre, cells - 1, 1))
            out.append(near - 6.0 * centre)
        return out

    def both(real, imag):
        shape = (8, cells)
        imag = jnp.where(row == 1, jnp.broadcast_to(imag, shape), 0.0)
        return jnp.where(row == 0, jnp.broadcast_to(real, shape), imag)

    exchange(1, field)
    for plane in range(1, depth + 1):
        turn(plane)
    eps = [spread(materials[plane : plane + 1], permittivity, 0) for plane in range(depth)]
    src = [spread(ports[plane : plane + 1], port_source, 1) for plane in range(depth)]
    finish(1)
    adjoint = []
    for plane, lap in enumerate(laplace(1, field)):
        real, imag = field[plane][0:1], field[plane][1:2]
        eps_re, eps_im = eps[plane]
        src_re, src_im = src[plane]
        local = both(
            wave_sq * (eps_re * real - eps_im * imag) - src_re,
            wave_sq * (eps_re * imag + eps_im * real) - src_im,
        )
        adjoint.append((lap + local) * norm_scale)
    exchange(2, adjoint)
    turn(0)
    turn(depth + 1)
    finish(2)
    for plane, lap in enumerate(laplace(2, adjoint)):
        real, imag = adjoint[plane][0:1], adjoint[plane][1:2]
        eps_re, eps_im = eps[plane]
        back = lap + both(
            wave_sq * (eps_re * real + eps_im * imag), wave_sq * (eps_re * imag - eps_im * real)
        )
        columns = back.T
        projection = head[...].astype(jnp.float32)
        d_hidden = columns[:, 0:1] * projection[0:1] + columns[:, 1:2] * projection[1:2]
        d_pre = d_hidden * factor[plane * cells : (plane + 1) * cells]
        d_pad[plane, grid_w : grid_w + cells] = d_pre.astype(jnp.bfloat16)

    ready = 0
    group_rows = 2 * line * rows
    for shift_z in range(3):
        left = turned[:, shift_z * cells : (shift_z + depth) * cells]
        for shift_y in range(3):
            top = (2 - shift_y) * grid_w
            first = 9 * shift_z + 3 * shift_y
            first = first * channels
            grad[first : first + wide] = jnp.dot(
                left,
                d_pad[:, top : top + cells].reshape(depth * cells, channels),
                preferred_element_type=jnp.float32,
            )
            while rows % 8 == 0 and ready < groups and (ready + 1) * group_rows <= first + wide:
                for slab in range(line):
                    pair_copy(ready, slab).start()
                ready += 1
    if rows % 8:
        for spot in range(groups * 2 * line):
            blocks[spot] = grad[spot * rows : (spot + 1) * rows]
        for group in range(groups):
            for slab in range(line):
                pair_copy(group, slab).start()

    group_order = list(range(1, groups)) + [0]
    line_order = list(range(1, line)) + [0]
    for k in group_order[:-1]:
        for j in line_order:
            slab = slab_at(j)
            group_out[k - 1, j] = widen(pair_sum(group_at(k), slab), padded)
            group_copy(k, j).start()
    total = None
    for j in line_order:
        slab = slab_at(j)
        total = pair_sum(mine, slab)
        for k in range(1, groups):
            group_copy(k, j).wait_recv()
            total = total + group_in[k - 1, j].astype(jnp.float32)[:rows]
        if j:
            line_out[j - 1] = widen(total, padded)
            line_copy(j).start()
    for j in range(1, line):
        line_copy(j).wait_recv()
        total = total + line_in[j - 1].astype(jnp.float32)[:rows]

    total = total * scale
    parts = width // 128
    for part in range(parts):
        narrow[pl.ds(part, rows, stride=parts), :] = total[:, part * 128 : part * 128 + 128]
    share = narrow[...]
    stepped = beta_one * moment[...] + (1.0 - beta_one) * share
    squared = beta_two * second[...] + (1.0 - beta_two) * share * share
    updated = master[...] - learn_rate * stepped / (jnp.sqrt(squared) + adam_eps)
    new_moment[...] = stepped
    new_second[...] = squared
    new_master[...] = updated
    narrow[...] = updated
    block = jnp.concatenate(
        [narrow[pl.ds(part, rows, stride=parts), :] for part in range(parts)], axis=1
    )
    full[mine, core, here] = widen(block, padded)

    for j in range(1, line):
        line_back(j).start()
    for k in range(1, groups):
        group_back(k, 0).start()
    pair_back(0, 0).start()
    for j in range(1, line):
        line_back(j).wait_recv()
        for k in range(1, groups):
            group_back(k, j).start()
        pair_back(0, j).start()
    for j in range(line):
        for k in range(1, groups):
            group_back(k, j).wait_recv()
            pair_back(k, j).start()
    for j in range(line):
        for k in range(groups):
            pair_back(k, j).wait_recv()
    for k in range(groups):
        for j in range(line):
            pair_copy(k, j).wait_send()
            pair_back(k, j).wait_send()
            if k:
                group_copy(k, j).wait_send()
                group_back(k, j).wait_send()
    for j in range(1, line):
        line_copy(j).wait_send()
        line_back(j).wait_send()


def whole_step(features, weights, head_proj, codes, tables, states):
    depth, grid_h, grid_w, channels = features.shape
    cells = grid_h * grid_w
    line = lax.axis_size("slab")
    groups = lax.axis_size("dp") // 2
    all_cells = depth * cells * groups * 2 * line
    scale = float(np.float32(1.0) / np.sqrt(np.float32(27 * channels)))
    norm_scale = float(np.float32(2.0) / np.sqrt(np.float32(all_cells)))
    rows_all = 27 * channels
    rows = rows_all // (groups * 2 * line)
    padded = -(-rows // 16) * 16
    flat = (rows * channels // 128, 128)
    tall = cells + 2 * grid_w
    spare = (groups * 2 * line, rows, channels) if rows % 8 else (1, 8, 128)
    vmem = pl.BlockSpec(memory_space=pltpu.VMEM)
    smem = pl.BlockSpec(memory_space=pltpu.SMEM)
    dma = pltpu.SemaphoreType.DMA
    state = jax.ShapeDtypeStruct(flat, jnp.float32)
    out = pl.pallas_call(
        functools.partial(step_kernel, (line, grid_w), scale, norm_scale),
        out_shape=[
            state,
            state,
            state,
            jax.ShapeDtypeStruct((groups, 2, line, padded, channels), jnp.bfloat16),
        ],
        in_specs=[vmem] * 5 + [smem] * 2 + [vmem] * 3,
        out_specs=[vmem] * 4,
        scratch_shapes=[
            pltpu.VMEM((rows_all, channels), jnp.float32),
            pltpu.VMEM(spare, jnp.float32),
            pltpu.VMEM((2, cells, channels), jnp.bfloat16),
            pltpu.VMEM((depth + 2, tall, 3 * channels), jnp.bfloat16),
            pltpu.VMEM((3 * channels, (depth + 2) * cells), jnp.bfloat16),
            pltpu.VMEM((depth * cells, channels), jnp.float32),
            pltpu.VMEM((depth, tall, channels), jnp.bfloat16),
            pltpu.VMEM((2, 2, 8, cells), jnp.float32),
            pltpu.VMEM((2, 2, 8, cells), jnp.float32),
            pltpu.VMEM((groups, line, rows, channels), jnp.float32),
            pltpu.VMEM((groups - 1, line, padded, channels), jnp.bfloat16),
            pltpu.VMEM((groups - 1, line, padded, channels), jnp.bfloat16),
            pltpu.VMEM((line - 1, padded, channels), jnp.bfloat16),
            pltpu.VMEM((line - 1, padded, channels), jnp.bfloat16),
            pltpu.VMEM(flat, jnp.float32),
            dma((3, 2)),
            dma((3, 2)),
            dma((groups, line)),
            dma((groups, line)),
            dma((groups - 1, line)),
            dma((groups - 1, line)),
            dma((line - 1,)),
            dma((line - 1,)),
            dma((line - 1,)),
            dma((line - 1,)),
            dma((groups - 1, line)),
            dma((groups - 1, line)),
            dma((groups, line)),
            dma((groups, line)),
        ],
        compiler_params=pltpu.CompilerParams(
            collective_id=0, has_side_effects=True, vmem_limit_bytes=36 * 1024 * 1024
        ),
    )(
        features.reshape(depth, cells, channels),
        weights,
        jnp.pad(head_proj.T, ((0, 14), (0, 0))),
        *[part.reshape(depth, cells) for part in codes],
        *tables,
        *[part.reshape(flat) for part in states],
    )
    full = out[3][:, :, :, :rows].reshape(weights.shape)
    return tuple(part.reshape(-1) for part in out[:3]) + (full,)


def body(
    features,
    kernel,
    head_proj,
    material_ids,
    port_ids,
    permittivity,
    port_source,
    master,
    moment,
    second,
):
    return whole_step(
        features[0],
        kernel,
        head_proj,
        (material_ids[0], port_ids[0]),
        (permittivity, port_source),
        (master, moment, second),
    )


def solution(mesh):
    placed = (
        P("dp", "slab", None, None, None),
        P(),
        P(),
        P("dp", "slab", None, None),
        P("dp", "slab", None, None),
        P(),
        P(),
        P(("dp", "slab")),
        P(("dp", "slab")),
        P(("dp", "slab")),
    )
    return jax.shard_map(
        body,
        mesh=mesh,
        in_specs=placed,
        out_specs=(P(("dp", "slab")), P(("dp", "slab")), P(("dp", "slab")), P()),
        check_vma=False,
    )
```
